32 devices in a mesh: leaf: 16 (over z, y, x), col: 2 (over core).
Axes of the slice: x: 2, y: 2, z: 4, core: 2. Of those that a mesh axis runs over, the one named last changes fastest.
Arguments:
- rows_a: bfloat16 [32768, 1024], P(('leaf', 'col')), may hold values from -0.125 to 0.125
- stair_counts: int32 [16, 8], P('leaf'), may hold values from 192 to 448, as said below
- block_maps: int32 [4, 8, 2, 2, 16], replicated, may hold values from 0 to 19, as said below
Outputs:
- factor: float32 [4, 16, 1280, 256], P(None, 'leaf', 'col')
- contribution: float32 [16, 1024, 1024], P('leaf', 'col')
The draws below stay inside these ranges and needn't reach their ends.
Inputs may be any that keep to these rules, and one draw needn't show every extreme that they name: Each row of stair_counts sums to 2048; in every row one count equals 192 and one equals 448. `block_maps`: for each level, front, child and index of col the 16 entries are distinct, and those of the two children together name every value below 20.
All inputs are finite; a program needn't handle non-finite values.
Results may differ from the reference program's by a relative error of at most 0.0003.
Values sent between devices are 32-bit elements; how exact they have to be, the bound alone decides.
A program may use at most 128 MiB of HBM per device.

```python
import jax
import jax.numpy as jnp
from jax import lax

W = 1024
KP = 256
SB = 32
STAIR = 8
LEVELS = 4
M = 2048
ROWS = 32768
WC = 512
PC = 128
FWC = 640
FW = 1280
CS = 16
PS = 20
FRONTS = 8
N_LEAF = 16
N_COL = 2


def draw_stair_counts(key, part):
    base = 3 * M // 32
    heavy_extra = M // 8
    spare = M - STAIR * base - heavy_extra
    skipped = jax.random.randint(jax.random.fold_in(key, 1), (N_LEAF, 1), 0, STAIR)
    offset = jax.random.randint(jax.random.fold_in(key, 4), (N_LEAF, 1), 1, STAIR)
    heavy = (skipped + offset) % STAIR
    lower = jnp.minimum(skipped, heavy)
    upper = jnp.maximum(skipped, heavy)
    picks = jax.random.randint(jax.random.fold_in(key, 2), (N_LEAF, spare), 0, STAIR - 2)
    picks = picks + (picks >= lower).astype(jnp.int32)
    picks = picks + (picks >= upper).astype(jnp.int32)
    columns = jnp.arange(STAIR, dtype=jnp.int32)
    onehot = (picks[:, :, None] == columns[None, None, :]).astype(jnp.int32)
    heavy_add = (heavy == columns[None, :]).astype(jnp.int32) * heavy_extra
    return (base + jnp.sum(onehot, axis=1) + heavy_add).astype(jnp.int32)


def one_front(key):
    subkeys = jax.random.split(key, 3)
    shuffled = jax.random.permutation(subkeys[0], PS)
    shared = jax.random.permutation(subkeys[1], CS)[:2 * CS - PS]
    second = jnp.concatenate([shuffled[CS:], shuffled[shared]])
    second = jax.random.permutation(subkeys[2], second)
    return jnp.stack([shuffled[:CS], second])


def draw_block_maps(key, part):
    subkeys = jax.random.split(jax.random.fold_in(key, 3), LEVELS * FRONTS * N_COL)
    front_maps = jax.vmap(one_front)(subkeys)
    return front_maps.reshape(LEVELS, FRONTS, N_COL, 2, CS).transpose(0, 1, 3, 2, 4).astype(jnp.int32)


def steps_of(key, dims, pieces, smallest, high):
    def one(position, shards_of):
        draws = jax.random.uniform(jax.random.fold_in(jax.random.fold_in(key, 6), position), (shards_of,), jnp.float32, smallest / len(pieces), high / len(pieces))
        return jnp.repeat(jnp.exp(draws), dims[position] // shards_of).reshape((-1,) + (1,) * (len(dims) - position - 1))

    factor_of = one(*pieces[0])
    for cut in pieces[1:]:
        factor_of = factor_of * one(*cut)
    return factor_of


def normal_values(rng, extent, spread, most, shards=(), kind=jnp.bfloat16):
    loudness = steps_of(rng, extent, shards, -0.22, 0.18) if shards else 1.0
    entries = jax.random.normal(rng, extent, jnp.float32) * spread * loudness
    return jnp.minimum(jnp.maximum(entries, -most), most).astype(kind)


def setup_inputs(seed: int = 0) -> dict:
    seeds = jax.random.split(jax.random.key(seed), 4)
    rows_a = normal_values(seeds[0], (ROWS, W), M ** -0.5, 0.125, ((0, 32),))
    stair_counts = draw_stair_counts(jax.random.fold_in(seeds[3], 71), 0)
    block_maps = draw_block_maps(jax.random.fold_in(seeds[3], 71), 0)
    return {"rows_a": rows_a, "stair_counts": stair_counts, "block_maps": block_maps}


def leaf_gram(a_leaf, counts):
    bounds = jnp.cumsum(counts)
    row_index = jnp.arange(M, dtype=jnp.int32)
    leading = jnp.sum((bounds[None, :] <= row_index[:, None]).astype(jnp.int32), axis=1)
    column_block = jnp.arange(W, dtype=jnp.int32) // (W // STAIR)
    masked = jnp.where(column_block[None, :] >= leading[:, None], a_leaf, jnp.zeros_like(a_leaf))
    return jnp.dot(masked.T.astype(jnp.float32), masked.astype(jnp.float32), preferred_element_type=jnp.float32)

def place_index(child_maps):
    device = jnp.arange(N_COL, dtype=jnp.int32)[:, None, None]
    within = jnp.arange(SB, dtype=jnp.int32)[None, None, :]
    return (device * FWC + child_maps[:, :, None] * SB + within).reshape(W).astype(jnp.int32)

def merge_front(first_child, second_child, front_maps):
    front = jnp.zeros((FW, FW), jnp.float32)
    first_index = place_index(front_maps[0])
    second_index = place_index(front_maps[1])
    front = front.at[first_index[:, None], first_index[None, :]].add(first_child)
    front = front.at[second_index[:, None], second_index[None, :]].add(second_child)
    device = jnp.arange(N_COL, dtype=jnp.int32)[:, None]
    pivot_index = (device * FWC + jnp.arange(PC, dtype=jnp.int32)[None, :]).reshape(KP)
    rest_index = (device * FWC + PC + jnp.arange(WC, dtype=jnp.int32)[None, :]).reshape(W)
    pivot_block = front[pivot_index][:, pivot_index]
    coupling = front[rest_index][:, pivot_index]
    corner = front[rest_index][:, rest_index]
    lower_factor = jnp.linalg.cholesky(pivot_block)
    upper_rows = jax.scipy.linalg.solve_triangular(lower_factor, coupling.T, lower=True).T
    schur = corner - jnp.dot(upper_rows, upper_rows.T, precision=lax.Precision.HIGHEST)
    factor_block = jnp.concatenate([lower_factor.reshape(N_COL, PC, KP), upper_rows.reshape(N_COL, WC, KP)], axis=1).reshape(FW, KP)
    return (schur, factor_block)

def reference(rows_a, stair_counts, block_maps):
    grams = lax.map(lambda pair: leaf_gram(pair[0], pair[1]), (rows_a.reshape(N_LEAF, M, W), stair_counts))
    current = grams
    levels_out = []
    for level_index in range(LEVELS):
        front_count = N_LEAF >> level_index + 1
        pairs = current.reshape(front_count, 2, W, W)
        level_maps = block_maps[level_index, :front_count]
        current, blocks = lax.map(lambda pair: merge_front(pair[0][0], pair[0][1], pair[1]), (pairs, level_maps))
        levels_out.append(jnp.repeat(blocks, 2 ** (level_index + 1), axis=0))
    factor = jnp.stack(levels_out)
    contribution = jnp.repeat(current, 2 ** LEVELS, axis=0)
    return (factor, contribution)
```

```python
import functools

import jax
import jax.numpy as jnp
from jax import lax
from jax.experimental import pallas as pl
from jax.experimental.pallas import tpu as pltpu
from jax.sharding import PartitionSpec as P

KP = 256
SB = 32
LEVELS = 4
T = 128
NB = 32
ROUND = 4
MESH = pl.DeviceIdType.MESH
F32 = jnp.float32
BF16 = jnp.bfloat16
VMEM_BYTES = 56 * 2**20


def split2(x):
    hi = x.astype(BF16)
    return hi, (x - hi.astype(F32)).astype(BF16)


def dot3(a, b, dims):
    (ah, al), (bh, bl) = a, b
    one = functools.partial(
        lax.dot_general, dimension_numbers=(dims, ((), ())), preferred_element_type=F32
    )
    return one(ah, bh) + (one(ah, bl) + one(al, bh))


def exact_dot(a, b, dims):
    return lax.dot_general(
        a, b, (dims, ((), ())), precision=lax.Precision.HIGHEST, preferred_element_type=F32
    )


def mirror_strip(ref, i):
    for k in range(i):
        ref[k * T : (k + 1) * T, i * T : (i + 1) * T] = ref[
            i * T : (i + 1) * T, k * T : (k + 1) * T
        ].T


def strip_of(ref, i):
    return ref.at[pl.ds(i * T, T), pl.ds(0, (i + 1) * T)]


def gram_kernel(strips, m_ref, out_ref, got, send_sem, recv_sem):
    leaf, col = lax.axis_index("leaf"), lax.axis_index("col")
    barrier = pltpu.get_barrier_semaphore()
    pl.semaphore_signal(barrier, inc=1, device_id=(leaf, 1 - col), device_id_type=MESH)
    part = got.at[0]
    land = got.at[1]
    copies = []
    for n, i in enumerate(reversed(range(strips))):
        part[i * T : (i + 1) * T, : (i + 1) * T] = lax.dot_general(
            m_ref[:, i * T : (i + 1) * T],
            m_ref[:, : (i + 1) * T],
            (((0,), (0,)), ((), ())),
            preferred_element_type=F32,
        )
        if n == 0:
            pl.semaphore_wait(barrier, 1)
        copy = pltpu.make_async_remote_copy(
            src_ref=strip_of(part, i),
            dst_ref=strip_of(land, i),
            send_sem=send_sem.at[i],
            recv_sem=recv_sem.at[i],
            device_id=(leaf, 1 - col),
            device_id_type=MESH,
        )
        copy.start()
        copies.append((i, copy))
    for i, copy in copies:
        copy.wait_recv()
        rows, cols = slice(i * T, (i + 1) * T), slice(0, (i + 1) * T)
        out_ref[rows, cols] = part[rows, cols] + land[rows, cols]
        mirror_strip(out_ref, i)
    for _, copy in copies:
        copy.wait_send()


def gram(masked, collective):
    width = masked.shape[1]
    strips = width // T
    return pl.pallas_call(
        functools.partial(gram_kernel, strips),
        out_shape=jax.ShapeDtypeStruct((width, width), F32),
        in_specs=[pl.BlockSpec(memory_space=pltpu.VMEM)],
        out_specs=pl.BlockSpec(memory_space=pltpu.VMEM),
        scratch_shapes=[
            pltpu.VMEM((2, width, width), F32),
            pltpu.SemaphoreType.DMA((strips,)),
            pltpu.SemaphoreType.DMA((strips,)),
        ],
        compiler_params=pltpu.CompilerParams(
            collective_id=collective, has_side_effects=True, vmem_limit_bytes=VMEM_BYTES
        ),
        name="gram",
    )(masked)


def exchange_kernel(strips, level, c_ref, out_ref, land, send_sem, recv_sem, fsend_sem, frecv_sem):
    leaf, col = lax.axis_index("leaf"), lax.axis_index("col")
    stride = 2**level
    bit = (leaf // stride) % 2
    partner = leaf + stride - 2 * stride * bit
    barrier = pltpu.get_barrier_semaphore()
    pl.semaphore_signal(barrier, inc=1, device_id=(partner, col), device_id_type=MESH)
    pl.semaphore_signal(barrier, inc=1, device_id=(leaf, 1 - col), device_id_type=MESH)
    pl.semaphore_wait(barrier, 2)
    orders = [
        [i for i in reversed(range(strips)) if (i % 4 in (0, 3)) == (core == 0)]
        for core in range(2)
    ]

    for core in range(2):

        @pl.when(col == core)
        def _():
            sends, forwards = [], []
            for i in orders[core]:
                copy = pltpu.make_async_remote_copy(
                    src_ref=strip_of(c_ref, i),
                    dst_ref=strip_of(land, i),
                    send_sem=send_sem.at[i],
                    recv_sem=recv_sem.at[i],
                    device_id=(partner, col),
                    device_id_type=MESH,
                )
                copy.start()
                sends.append(copy)
            theirs = []
            for i in orders[1 - core]:
                theirs.append(
                    pltpu.make_async_remote_copy(
                        src_ref=strip_of(land, i),
                        dst_ref=strip_of(land, i),
                        send_sem=fsend_sem.at[i],
                        recv_sem=frecv_sem.at[i],
                        device_id=(leaf, 1 - col),
                        device_id_type=MESH,
                    )
                )
            for n, i in enumerate(orders[core]):
                sends[n].wait_recv()
                forward = pltpu.make_async_remote_copy(
                    src_ref=strip_of(land, i),
                    dst_ref=strip_of(land, i),
                    send_sem=fsend_sem.at[i],
                    recv_sem=frecv_sem.at[i],
                    device_id=(leaf, 1 - col),
                    device_id_type=MESH,
                )
                forward.start()
                forwards.append(forward)
                out_ref[i * T : (i + 1) * T, : (i + 1) * T] = land[
                    i * T : (i + 1) * T, : (i + 1) * T
                ]
                mirror_strip(out_ref, i)
                if n:
                    j = orders[1 - core][n - 1]
                    theirs[n - 1].wait_recv()
                    out_ref[j * T : (j + 1) * T, : (j + 1) * T] = land[
                        j * T : (j + 1) * T, : (j + 1) * T
                    ]
                    mirror_strip(out_ref, j)
            j = orders[1 - core][-1]
            theirs[-1].wait_recv()
            out_ref[j * T : (j + 1) * T, : (j + 1) * T] = land[
                j * T : (j + 1) * T, : (j + 1) * T
            ]
            mirror_strip(out_ref, j)
            for copy in sends + forwards:
                copy.wait_send()


def exchange(current, level, collective):
    width = current.shape[0]
    strips = width // T
    return pl.pallas_call(
        functools.partial(exchange_kernel, strips, level),
        out_shape=jax.ShapeDtypeStruct((width, width), F32),
        in_specs=[pl.BlockSpec(memory_space=pltpu.VMEM)],
        out_specs=pl.BlockSpec(memory_space=pltpu.VMEM),
        scratch_shapes=[pltpu.VMEM((width, width), F32)]
        + [pltpu.SemaphoreType.DMA((strips,)) for _ in range(4)],
        compiler_params=pltpu.CompilerParams(
            collective_id=collective, has_side_effects=True, vmem_limit_bytes=VMEM_BYTES
        ),
        name="exchange",
    )(current)


def factor_small(diag):
    row = lax.broadcasted_iota(jnp.int32, (NB, T), 0)
    lane = lax.broadcasted_iota(jnp.int32, (NB, T), 1)
    m = jnp.where(lane < NB, diag, jnp.where(lane == row + NB, 1.0, 0.0))
    for j in range(0, NB, ROUND):
        cols = [jnp.broadcast_to(m[:, j + q : j + q + 1], (NB, T)) for q in range(ROUND)]
        rows = [m[j + p : j + p + 1, :] for p in range(ROUND)]
        b = [[cols[q][j + p : j + p + 1, :] for q in range(ROUND)] for p in range(ROUND)]
        update = m
        for q in range(ROUND):
            r = 1.0 / b[q][q]
            factor = cols[q] * r
            update = update - factor * rows[q]
            for t in range(q + 1, ROUND):
                cols[t] = cols[t] - factor * b[q][t]
            for p in range(q + 1, ROUND):
                g = b[p][q] * r
                rows[p] = rows[p] - g * rows[q]
                for t in range(q + 1, ROUND):
                    b[p][t] = b[p][t] - g * b[q][t]
        m_next = jnp.where(row >= j + ROUND, update, m)
        for p in range(1, ROUND):
            m_next = jnp.where(row == j + p, rows[p], m_next)
        m = m_next
    pivots = jnp.sum(jnp.where(lane == row, m, 0.0), axis=1, keepdims=True)
    inverse = pltpu.roll(m, T - NB, 1) * lax.rsqrt(pivots)
    return inverse[:, :NB]


def front_kernel(
    strips, last, idx_ref, own_ref, other_ref, factor_ref, next_ref, front, work, upper, low, u, uh, ul
):
    subs = front.shape[0] // SB
    per = T // SB
    pivot_tiles = KP // T
    tiles = front.shape[1] // T
    lane_group = lax.broadcasted_iota(jnp.int32, (SB, T), 1) // SB

    def entry(child, field, s):
        return idx_ref[(child * 5 + field) * subs + s]

    def assemble(r, tile_count):
        base = pl.multiple_of(r * SB, SB)
        for child, ref in ((0, own_ref), (1, other_ref)):
            present = entry(child, 1, r) > 0

            @pl.when(present)
            def _():
                start = pl.multiple_of(entry(child, 0, r) * SB, SB)
                for t in range(tile_count):
                    if child:
                        total = front[pl.ds(base, SB), t * T : (t + 1) * T]
                    else:
                        total = jnp.zeros((SB, T), F32)
                    for q in range(per):
                        s = t * per + q
                        tile = ref[
                            pl.ds(start, SB),
                            pl.ds(pl.multiple_of(entry(child, 2, s) * T, T), T),
                        ]
                        moved = pltpu.roll(tile, entry(child, 3, s), 1)
                        picked = jnp.where(lane_group == entry(child, 4, s), moved, 0.0)
                        total = total + picked
                    front[pl.ds(base, SB), t * T : (t + 1) * T] = total

            if not child:

                @pl.when(jnp.logical_not(present))
                def _():
                    front[pl.ds(base, SB), : tile_count * T] = jnp.zeros(
                        (SB, tile_count * T), F32
                    )

    @pl.loop(0, KP // SB)
    def _(r):
        assemble(r, pivot_tiles)

    @pl.loop(KP // SB, subs)
    def _(r):
        assemble(r, tiles)

    work[...] = front[:KP, :KP]
    lanes = lax.broadcasted_iota(jnp.int32, (NB, KP), 1)
    rows32 = lax.broadcasted_iota(jnp.int32, (NB, KP), 0)
    for b in range(KP // NB):
        lo = b * NB
        panel = work[lo : lo + NB, :]
        tile = lo // T
        diag = panel[:, tile * T : (tile + 1) * T]
        if lo % T:
            diag = pltpu.roll(diag, T - lo % T, 1)
        w = factor_small(diag)
        in_diag = (lanes >= lo) & (lanes < lo + NB)
        opened = jnp.where(in_diag, jnp.where(lanes == rows32 + lo, 1.0, 0.0), panel)
        q = exact_dot(w, opened, ((1,), (0,)))
        r_diag = exact_dot(w, jnp.where(in_diag, panel, 0.0), ((1,), (0,)))
        upper[lo : lo + NB, :] = jnp.where(
            lanes < lo + NB, jnp.where(lanes >= rows32 + lo, r_diag, 0.0), q
        )
        low[lo : lo + NB, :] = jnp.where(lanes <= rows32 + lo, q, 0.0)
        if lo + NB < KP:
            below = lo + NB
            right = jnp.where(lanes >= below, q, 0.0)
            change = exact_dot(right, q, ((0,), (0,)))
            lanes_b = lax.broadcasted_iota(jnp.int32, (KP - below, KP), 1)
            rest = work[below:, :]
            rest = jnp.where((lanes_b >= lo) & (lanes_b < below), 0.0, rest)
            work[below:, :] = rest - change[below:, :]

    col = lax.axis_index("col")
    share = KP // 2
    work[...] = upper[...].T
    factor_ref[:share, :] = work[pl.ds(pl.multiple_of(col * share, share), share), :]
    inverse = split2(low[...])

    @pl.loop(0, strips)
    def _(i):
        base = pl.multiple_of(i * T, T)
        coupling = front[pl.ds(pl.multiple_of(KP + base, T), T), :KP]
        strip = dot3(split2(coupling), inverse, ((1,), (1,)))
        u[pl.ds(base, T), :] = strip
        hi, lo = split2(strip)
        uh[pl.ds(base, T), :] = hi
        ul[pl.ds(base, T), :] = lo

    half = strips * T // 2
    factor_ref[share:, :] = u[pl.ds(pl.multiple_of(col * half, half), half), :]
    offset = col * half if last else 0
    whole = (uh[...], ul[...])

    @pl.loop(0, strips // 2 if last else strips)
    def _(i):
        base = pl.multiple_of(i * T, T)
        at = pl.multiple_of(base + offset, T)
        product = dot3((uh[pl.ds(at, T), :], ul[pl.ds(at, T), :]), whole, ((1,), (1,)))
        next_ref[pl.ds(base, T), :] = front[pl.ds(pl.multiple_of(at + KP, T), T), KP:] - product


def merge(own, other, index, last):
    width = own.shape[0]
    front_width = width + KP
    out_rows = width // 2 if last else width
    vmem = pl.BlockSpec(memory_space=pltpu.VMEM)
    return pl.pallas_call(
        functools.partial(front_kernel, width // T, last),
        out_shape=(
            jax.ShapeDtypeStruct((front_width // 2, KP), F32),
            jax.ShapeDtypeStruct((out_rows, width), F32),
        ),
        in_specs=[pl.BlockSpec(memory_space=pltpu.SMEM), vmem, vmem],
        out_specs=(vmem, vmem),
        scratch_shapes=[
            pltpu.VMEM((front_width, front_width), F32),
            pltpu.VMEM((KP, KP), F32),
            pltpu.VMEM((KP, KP), F32),
            pltpu.VMEM((KP, KP), F32),
            pltpu.VMEM((width, KP), F32),
            pltpu.VMEM((width, KP), BF16),
            pltpu.VMEM((width, KP), BF16),
        ],
        compiler_params=pltpu.CompilerParams(vmem_limit_bytes=VMEM_BYTES),
        name="front",
    )(index, own, other)


def index_table(child_maps, sub_count):
    col_count, child_subs = child_maps.shape
    per = T // SB
    pivot_subs = KP // col_count // SB
    matches = (child_maps[:, :, None] == lax.iota(jnp.int32, sub_count)[None, None, :]).astype(
        jnp.int32
    )
    offset = lax.iota(jnp.int32, col_count)[:, None] * child_subs
    source = jnp.sum(matches * lax.iota(jnp.int32, child_subs)[None, :, None], axis=1) + offset
    present = jnp.sum(matches, axis=1)

    def pivots_first(table):
        return jnp.concatenate(
            [table[:, :pivot_subs].reshape(-1), table[:, pivot_subs:].reshape(-1)]
        )

    source, present = pivots_first(source), pivots_first(present)
    place = lax.iota(jnp.int32, source.shape[0]) % per
    shift = (place - source % per + per) % per * SB
    group = jnp.where(present > 0, place, -1)
    return jnp.concatenate([source, present, source // per, shift, group])


def body(rows_a, stair_counts, block_maps):
    col_count = lax.axis_size("col")
    col_index = lax.axis_index("col")
    leaf_index = lax.axis_index("leaf")
    local_rows, width = rows_a.shape
    front_cols = (width + KP) // col_count
    sub_count = front_cols // SB
    bounds = jnp.cumsum(stair_counts[0])
    row_index = col_index * local_rows + lax.iota(jnp.int32, local_rows)
    leading = jnp.sum((bounds[None, :] <= row_index[:, None]).astype(jnp.int32), axis=1)
    column_block = lax.iota(jnp.int32, width) // (width // stair_counts.shape[1])
    masked = jnp.where(column_block[None, :] >= leading[:, None], rows_a, jnp.zeros_like(rows_a))
    current = gram(masked, 0)
    factors = []
    for level in range(LEVELS):
        other = exchange(current, level, level + 1)
        pair_bit = leaf_index >> level & 1
        front_maps = lax.dynamic_index_in_dim(
            block_maps[level], leaf_index >> level + 1, 0, keepdims=False
        )
        own_maps = lax.dynamic_index_in_dim(front_maps, pair_bit, 0, keepdims=False)
        other_maps = lax.dynamic_index_in_dim(front_maps, 1 - pair_bit, 0, keepdims=False)
        index = jnp.concatenate(
            [index_table(own_maps, sub_count), index_table(other_maps, sub_count)]
        )
        factor, current = merge(current, other, index, level == LEVELS - 1)
        factors.append(factor)
    return (jnp.stack(factors)[:, None], current[None])


def solution(mesh):
    return jax.shard_map(
        body,
        mesh=mesh,
        in_specs=(P(("leaf", "col"), None), P("leaf", None), P()),
        out_specs=(P(None, "leaf", "col", None), P("leaf", "col", None)),
        check_vma=False,
    )
```

```python
import functools

import jax
import jax.numpy as jnp
from jax import lax
from jax.experimental import pallas as pl
from jax.experimental.pallas import tpu as pltpu
from jax.sharding import PartitionSpec as P

KP = 256
SB = 32
LEVELS = 4
T = 128
G = 256
NB = 32
ROUND = 4
MESH = pl.DeviceIdType.MESH
F32 = jnp.float32
BF16 = jnp.bfloat16
VMEM_BYTES = 56 * 2**20


def split2(x):
    hi = x.astype(BF16)
    return hi, (x - hi.astype(F32)).astype(BF16)


def dot3(a, b, dims):
    (ah, al), (bh, bl) = a, b
    one = functools.partial(
        lax.dot_general, dimension_numbers=(dims, ((), ())), preferred_element_type=F32
    )
    return one(ah, bh) + (one(ah, bl) + one(al, bh))


def exact_dot(a, b, dims):
    return lax.dot_general(
        a, b, (dims, ((), ())), precision=lax.Precision.HIGHEST, preferred_element_type=F32
    )


def mirror_strip(ref, i):
    for k in range(i):
        ref[k * T : (k + 1) * T, i * T : (i + 1) * T] = ref[
            i * T : (i + 1) * T, k * T : (k + 1) * T
        ].T


def strip_of(ref, i):
    return ref.at[pl.ds(i * T, T), pl.ds(0, (i + 1) * T)]


def gram_kernel(strips, m_ref, out_ref, got, send_sem, recv_sem):
    leaf, col = lax.axis_index("leaf"), lax.axis_index("col")
    barrier = pltpu.get_barrier_semaphore()
    pl.semaphore_signal(barrier, inc=1, device_id=(leaf, 1 - col), device_id_type=MESH)
    part = got.at[0]
    land = got.at[1]
    copies = []
    for n, i in enumerate(reversed(range(strips))):
        part[i * T : (i + 1) * T, : (i + 1) * T] = lax.dot_general(
            m_ref[:, i * T : (i + 1) * T],
            m_ref[:, : (i + 1) * T],
            (((0,), (0,)), ((), ())),
            preferred_element_type=F32,
        )
        if n == 0:
            pl.semaphore_wait(barrier, 1)
        copy = pltpu.make_async_remote_copy(
            src_ref=strip_of(part, i),
            dst_ref=strip_of(land, i),
            send_sem=send_sem.at[i],
            recv_sem=recv_sem.at[i],
            device_id=(leaf, 1 - col),
            device_id_type=MESH,
        )
        copy.start()
        copies.append((i, copy))
    for i, copy in copies:
        copy.wait_recv()
        rows, cols = slice(i * T, (i + 1) * T), slice(0, (i + 1) * T)
        out_ref[rows, cols] = part[rows, cols] + land[rows, cols]
        mirror_strip(out_ref, i)
    for _, copy in copies:
        copy.wait_send()


def gram(masked, collective):
    width = masked.shape[1]
    strips = width // T
    return pl.pallas_call(
        functools.partial(gram_kernel, strips),
        out_shape=jax.ShapeDtypeStruct((width, width), F32),
        in_specs=[pl.BlockSpec(memory_space=pltpu.VMEM)],
        out_specs=pl.BlockSpec(memory_space=pltpu.VMEM),
        scratch_shapes=[
            pltpu.VMEM((2, width, width), F32),
            pltpu.SemaphoreType.DMA((strips,)),
            pltpu.SemaphoreType.DMA((strips,)),
        ],
        compiler_params=pltpu.CompilerParams(
            collective_id=collective, has_side_effects=True, vmem_limit_bytes=VMEM_BYTES
        ),
        name="gram",
    )(masked)


def pieces_of(quarter, strips):
    cut = []
    for k in range(quarter, strips // 2, 4):
        for i in (strips - 1 - k, k):
            for at in range(0, i + 1, 2):
                cut.append((i, at, min(2, i + 1 - at)))
    return cut


def exchange_kernel(strips, level, c_ref, out_ref, send_sem, recv_sem):
    leaf, col = lax.axis_index("leaf"), lax.axis_index("col")
    side = leaf % 2
    stride = 2**level
    bit = (leaf // stride) % 2
    relay = level == LEVELS - 1
    split = level > 0
    cuts = [pieces_of(quarter, strips) for quarter in range(4)]
    count = len(cuts[0])
    beside = (leaf + 1 - 2 * side, col)
    sibling = (leaf, 1 - col)
    if relay:
        near = stride // 2
        near_bit = (leaf // near) % 2
        inner = bit + near_bit == 1
        partner = (leaf + near - 2 * near * bit, col)
        outer = (leaf + near - 2 * near * near_bit, col)
    else:
        partner = (leaf + stride - 2 * stride * bit, col)

    barrier = pltpu.get_barrier_semaphore()

    def greet(device):
        pl.semaphore_signal(barrier, inc=1, device_id=device, device_id_type=MESH)

    greet(sibling)
    if split:
        greet(beside)
    if relay:
        greet(outer)

        @pl.when(inner)
        def _():
            greet(partner)
            pl.semaphore_wait(barrier, 4)

        @pl.when(jnp.logical_not(inner))
        def _():
            pl.semaphore_wait(barrier, 3)

    else:
        greet(partner)
        pl.semaphore_wait(barrier, 3 if split else 2)

    def copy_of(kind, quarter, n, source, device):
        i, at, blocks = cuts[quarter][n]
        place = (pl.ds(i * T, T), pl.ds(at * T, blocks * T))
        return pltpu.make_async_remote_copy(
            src_ref=source.at[place],
            dst_ref=out_ref.at[place],
            send_sem=send_sem.at[kind, quarter, n],
            recv_sem=recv_sem.at[quarter, n],
            device_id=device,
            device_id_type=MESH,
        )

    def mirror(quarter, n):
        i, at, blocks = cuts[quarter][n]
        for k in range(at, min(at + blocks, i)):
            out_ref[k * T : (k + 1) * T, i * T : (i + 1) * T] = out_ref[
                i * T : (i + 1) * T, k * T : (k + 1) * T
            ].T

    def cross(quarter, n):
        return copy_of(0, quarter, n, c_ref, partner)

    def to_sibling(quarter, n):
        return copy_of(1, quarter, n, out_ref, sibling)

    def to_beside(quarter, n):
        return copy_of(2, quarter, n, out_ref, beside)

    def to_outer(quarter, n):
        return copy_of(3, quarter, n, out_ref, outer)

    def role(core, half):
        mine = [2 * half + core] if split else [core, 2 + core]
        nexts = [2 * (1 - half) + core] if split else []
        theirs = [1 - core, 3 - core]
        order = [(quarter, n) for n in range(count) for quarter in mine]

        def send_all():
            for quarter, n in order:
                cross(quarter, n).start()

        if relay:
            pl.when(inner)(send_all)
        else:
            send_all()
        for n in range(count):
            for quarter in mine:
                cross(quarter, n).wait_recv()
                if relay:

                    @pl.when(inner)
                    def _():
                        to_outer(quarter, n).start()

                if split:
                    to_beside(quarter, n).start()
                to_sibling(quarter, n).start()
            for quarter in mine:
                mirror(quarter, n)
            if n:
                for quarter in nexts:
                    to_beside(quarter, n - 1).wait_recv()
                    to_sibling(quarter, n - 1).start()
                    mirror(quarter, n - 1)
            if n > 1:
                for quarter in theirs:
                    to_sibling(quarter, n - 2).wait_recv()
                    mirror(quarter, n - 2)
        for quarter in nexts:
            to_beside(quarter, count - 1).wait_recv()
            to_sibling(quarter, count - 1).start()
            mirror(quarter, count - 1)
        for n in range(count - 2, count):
            for quarter in theirs:
                to_sibling(quarter, n).wait_recv()
                mirror(quarter, n)

        def crossed():
            for quarter, n in order:
                cross(quarter, n).wait_send()
                if relay:
                    to_outer(quarter, n).wait_send()

        if relay:
            pl.when(inner)(crossed)
        else:
            crossed()
        for n in range(count):
            for quarter in mine:
                if split:
                    to_beside(quarter, n).wait_send()
            for quarter in mine + nexts:
                to_sibling(quarter, n).wait_send()

    for core in range(2):
        for half in range(2) if split else [0]:
            chosen = (col == core) & (side == half) if split else col == core
            pl.when(chosen)(functools.partial(role, core, half))


def exchange(current, level, collective):
    width = current.shape[0]
    strips = width // T
    return pl.pallas_call(
        functools.partial(exchange_kernel, strips, level),
        out_shape=jax.ShapeDtypeStruct((width, width), F32),
        in_specs=[pl.BlockSpec(memory_space=pltpu.VMEM)],
        out_specs=pl.BlockSpec(memory_space=pltpu.VMEM),
        scratch_shapes=[
            pltpu.SemaphoreType.DMA((4, 4, len(pieces_of(0, strips)))),
            pltpu.SemaphoreType.DMA((4, len(pieces_of(0, strips)))),
        ],
        compiler_params=pltpu.CompilerParams(
            collective_id=collective, has_side_effects=True, vmem_limit_bytes=VMEM_BYTES
        ),
        name="exchange",
    )(current)


def factor_small(diag):
    row = lax.broadcasted_iota(jnp.int32, (NB, T), 0)
    lane = lax.broadcasted_iota(jnp.int32, (NB, T), 1)
    m = jnp.where(lane < NB, diag, jnp.where(lane == row + NB, 1.0, 0.0))
    for j in range(0, NB, ROUND):
        cols = [jnp.broadcast_to(m[:, j + q : j + q + 1], (NB, T)) for q in range(ROUND)]
        rows = [m[j + p : j + p + 1, :] for p in range(ROUND)]
        b = [[cols[q][j + p : j + p + 1, :] for q in range(ROUND)] for p in range(ROUND)]
        update = m
        for q in range(ROUND):
            r = 1.0 / b[q][q]
            factor = cols[q] * r
            update = update - factor * rows[q]
            for t in range(q + 1, ROUND):
                cols[t] = cols[t] - factor * b[q][t]
            for p in range(q + 1, ROUND):
                g = b[p][q] * r
                rows[p] = rows[p] - g * rows[q]
                for t in range(q + 1, ROUND):
                    b[p][t] = b[p][t] - g * b[q][t]
        m_next = jnp.where(row >= j + ROUND, update, m)
        for p in range(1, ROUND):
            m_next = jnp.where(row == j + p, rows[p], m_next)
        m = m_next
    pivots = jnp.sum(jnp.where(lane == row, m, 0.0), axis=1, keepdims=True)
    inverse = pltpu.roll(m, T - NB, 1) * lax.rsqrt(pivots)
    return inverse[:, :NB]


def front_kernel(
    level, last, idx_ref, own_ref, other_ref, factor_ref, next_ref, front, work, upper, low, u, uh, ul, *full
):
    width = own_ref.shape[0]
    groups = width // G
    subs = front.shape[0] // SB
    per = T // SB
    pivot_tiles = KP // T
    lane_group = lax.broadcasted_iota(jnp.int32, (SB, T), 1) // SB

    def entry(child, field, s):
        return idx_ref[((level * 2 + child) * 5 + field) * subs + s]

    def assemble(r, tile_count):
        base = pl.multiple_of(r * SB, SB)
        for child, ref in ((0, own_ref), (1, other_ref)):
            present = entry(child, 1, r) > 0

            @pl.when(present)
            def _():
                start = pl.multiple_of(entry(child, 0, r) * SB, SB)
                for t in range(tile_count):
                    if child:
                        total = front[pl.ds(base, SB), t * T : (t + 1) * T]
                    else:
                        total = jnp.zeros((SB, T), F32)
                    for q in range(per):
                        s = t * per + q
                        tile = ref[
                            pl.ds(start, SB),
                            pl.ds(pl.multiple_of(entry(child, 2, s) * T, T), T),
                        ]
                        moved = pltpu.roll(tile, entry(child, 3, s), 1)
                        picked = jnp.where(lane_group == entry(child, 4, s), moved, 0.0)
                        total = total + picked
                    front[pl.ds(base, SB), t * T : (t + 1) * T] = total

            if not child:

                @pl.when(jnp.logical_not(present))
                def _():
                    front[pl.ds(base, SB), : tile_count * T] = jnp.zeros(
                        (SB, tile_count * T), F32
                    )

    @pl.loop(0, KP // SB)
    def _(r):
        assemble(r, pivot_tiles)

    for g in range(groups):

        @pl.loop((KP + g * G) // SB, (KP + (g + 1) * G) // SB)
        def _(r):
            assemble(r, (KP + (g + 1) * G) // T)

    work[...] = front[:KP, :KP]
    lanes = lax.broadcasted_iota(jnp.int32, (NB, KP), 1)
    rows32 = lax.broadcasted_iota(jnp.int32, (NB, KP), 0)
    for b in range(KP // NB):
        lo = b * NB
        panel = work[lo : lo + NB, :]
        tile = lo // T
        diag = panel[:, tile * T : (tile + 1) * T]
        if lo % T:
            diag = pltpu.roll(diag, T - lo % T, 1)
        w = factor_small(diag)
        in_diag = (lanes >= lo) & (lanes < lo + NB)
        opened = jnp.where(in_diag, jnp.where(lanes == rows32 + lo, 1.0, 0.0), panel)
        q = exact_dot(w, opened, ((1,), (0,)))
        r_diag = exact_dot(w, jnp.where(in_diag, panel, 0.0), ((1,), (0,)))
        upper[lo : lo + NB, :] = jnp.where(
            lanes < lo + NB, jnp.where(lanes >= rows32 + lo, r_diag, 0.0), q
        )
        low[lo : lo + NB, :] = jnp.where(lanes <= rows32 + lo, q, 0.0)
        if lo + NB < KP:
            below = lo + NB
            right = jnp.where(lanes >= below, q, 0.0)
            change = exact_dot(right, q, ((0,), (0,)))
            lanes_b = lax.broadcasted_iota(jnp.int32, (KP - below, KP), 1)
            rest = work[below:, :]
            rest = jnp.where((lanes_b >= lo) & (lanes_b < below), 0.0, rest)
            work[below:, :] = rest - change[below:, :]

    col = lax.axis_index("col")
    share = KP // 2
    work[...] = upper[...].T
    factor_ref[:share, :] = work[pl.ds(pl.multiple_of(col * share, share), share), :]
    inverse = split2(low[...])

    result = full[0] if last else next_ref
    for g in range(groups):
        lo, hi = g * G, (g + 1) * G
        strip = dot3(split2(front[KP + lo : KP + hi, :KP]), inverse, ((1,), (1,)))
        u[lo:hi, :] = strip
        uh[lo:hi, :], ul[lo:hi, :] = split2(strip)
    for g in range(groups):
        lo, hi = g * G, (g + 1) * G
        product = dot3(
            (uh[lo:hi, :], ul[lo:hi, :]), (uh[:hi, :], ul[:hi, :]), ((1,), (1,))
        )
        result[lo:hi, :hi] = front[KP + lo : KP + hi, KP : KP + hi] - product
        for k in range(g):
            result[k * G : (k + 1) * G, lo:hi] = result[lo:hi, k * G : (k + 1) * G].T

    half = width // 2
    own_half = pl.ds(pl.multiple_of(col * half, half), half)
    factor_ref[share:, :] = u[own_half, :]
    if last:
        next_ref[...] = result[own_half, :]


def merge(own, other, index, level):
    width = own.shape[0]
    front_width = width + KP
    last = level == LEVELS - 1
    out_rows = width // 2 if last else width
    vmem = pl.BlockSpec(memory_space=pltpu.VMEM)
    return pl.pallas_call(
        functools.partial(front_kernel, level, last),
        out_shape=(
            jax.ShapeDtypeStruct((front_width // 2, KP), F32),
            jax.ShapeDtypeStruct((out_rows, width), F32),
        ),
        in_specs=[pl.BlockSpec(memory_space=pltpu.SMEM), vmem, vmem],
        out_specs=(vmem, vmem),
        scratch_shapes=[
            pltpu.VMEM((front_width, front_width), F32),
            pltpu.VMEM((KP, KP), F32),
            pltpu.VMEM((KP, KP), F32),
            pltpu.VMEM((KP, KP), F32),
            pltpu.VMEM((width, KP), F32),
            pltpu.VMEM((width, KP), BF16),
            pltpu.VMEM((width, KP), BF16),
        ]
        + ([pltpu.VMEM((width, width), F32)] if last else []),
        compiler_params=pltpu.CompilerParams(vmem_limit_bytes=VMEM_BYTES),
        name="front",
    )(index, own, other)


def index_table(child_maps, sub_count):
    col_count, child_subs = child_maps.shape[-2:]
    per = T // SB
    pivot_subs = KP // col_count // SB
    matches = child_maps[..., :, None] == lax.iota(jnp.int32, sub_count)
    offset = lax.iota(jnp.int32, col_count)[:, None] * child_subs
    names = lax.iota(jnp.int32, child_subs)[:, None] + 1
    found = jnp.sum(jnp.where(matches, names, 0), axis=-2)
    coded = jnp.where(found > 0, found + offset, 0)
    parts = [coded[:, :, c, :pivot_subs] for c in range(col_count)]
    parts += [coded[:, :, c, pivot_subs:] for c in range(col_count)]
    coded = jnp.concatenate(parts, axis=-1)
    present = (coded > 0).astype(jnp.int32)
    source = jnp.maximum(coded - 1, 0)
    place = lax.broadcasted_iota(jnp.int32, coded.shape, 2) % per
    shift = (place - source % per + per) % per * SB
    group = jnp.where(present > 0, place, -1)
    return jnp.stack([source, present, source // per, shift, group], axis=2).reshape(-1)


def body(rows_a, stair_counts, block_maps):
    col_count = lax.axis_size("col")
    col_index = lax.axis_index("col")
    leaf_index = lax.axis_index("leaf")
    local_rows, width = rows_a.shape
    front_cols = (width + KP) // col_count
    sub_count = front_cols // SB
    bounds = jnp.cumsum(stair_counts[0])
    row_index = col_index * local_rows + lax.iota(jnp.int32, local_rows)
    leading = jnp.sum((bounds[None, :] <= row_index[:, None]).astype(jnp.int32), axis=1)
    column_block = lax.iota(jnp.int32, width) // (width // stair_counts.shape[1])
    masked = jnp.where(column_block[None, :] >= leading[:, None], rows_a, jnp.zeros_like(rows_a))
    current = gram(masked, 0)
    chosen = []
    for level in range(LEVELS):
        front_maps = lax.dynamic_index_in_dim(
            block_maps[level], leaf_index >> level + 1, 0, keepdims=False
        )
        chosen.append(jnp.where((leaf_index >> level & 1) == 0, front_maps, front_maps[::-1]))
    index = index_table(jnp.stack(chosen), sub_count)
    factors = []
    for level in range(LEVELS):
        other = exchange(current, level, level + 1)
        factor, current = merge(current, other, index, level)
        factors.append(factor)
    return (jnp.stack(factors)[:, None], current[None])


def solution(mesh):
    return jax.shard_map(
        body,
        mesh=mesh,
        in_specs=(P(("leaf", "col"), None), P("leaf", None), P()),
        out_specs=(P(None, "leaf", "col", None), P("leaf", "col", None)),
        check_vma=False,
    )
```
